256 devices in a mesh: alpha: 16 (over y_hi, z), beta: 4 (over y_lo, core), task: 4 (over x).
Axes of the slice: x: 4, y: 4 (y_hi: 2, y_lo: 2; y = y_hi * 2 + y_lo), z: 8, core: 2. Of those that a mesh axis runs over, the one named last changes fastest.
Arguments:
- vector: float32 [4096, 4096], P('alpha', 'beta'), may hold values from -6 to 6
- op_alpha: float32 [4, 4096, 4096], P('task', 'alpha'), may hold values from -2 to 2, as said below
- op_beta: float32 [4, 4096, 4096], P('task', 'beta'), may hold values from -2 to 2, as said below
- op_weight: float32 [4], replicated, may hold values from 0.5 to 2
- alpha_string: int32 [4096], P('alpha'), may hold values from 0 to 65535
- beta_string: int32 [4096], P('beta'), may hold values from 0 to 65535
- alpha_energy: float32 [65536], replicated, may hold values from -4 to 4
- beta_energy: float32 [65536], replicated, may hold values from -4 to 4
Outputs:
- sigma: float32 [4096, 4096], P('alpha', ('beta', 'task'))
The draws below stay inside these ranges and needn't reach their ends.
Inputs may be any that keep to these rules, and one draw needn't show every extreme that they name: Every op_alpha[k] is a symmetric matrix. Every op_beta[k] is a symmetric matrix.
All inputs are finite; a program needn't handle non-finite values.
Results may differ from the reference program's by a relative error of at most 0.0001.
Values sent between devices are 32-bit elements; how exact they have to be, the bound alone decides.
No kernel may reach another device: no remote copies, remote signals or barrier semaphores. Data moves between devices by JAX's collectives and lax.ppermute only.
A program may use at most 128 MiB of HBM per device.

```python
import math
import jax
import jax.numpy as jnp
from jax import lax

STR = 65536
NA = 4096
NB = 4096
K = 4


def symmetric_stack(key, amount, order):
    raw = jnp.clip(jax.random.normal(key, (amount, order, order), jnp.float32), -4.0, 4.0)
    return (raw + jnp.swapaxes(raw, 1, 2)) * (0.70710678 / jnp.sqrt(jnp.float32(order)))


def draw_op_alpha(key, part):
    return symmetric_stack(jax.random.fold_in(key, 11), K, NA)


def draw_op_beta(key, part):
    return symmetric_stack(jax.random.fold_in(key, 23), K, NB)


def with_ends(drawn, key, smallest, high):
    longest = drawn.shape.index(max(drawn.shape))
    spots = []
    for shift in (0, 1):
        where = [jax.random.randint(jax.random.fold_in(key, axis), (), 0, length) for axis, length in enumerate(drawn.shape)]
        where[longest] = (where[longest] + shift) % drawn.shape[longest]
        spots.append(tuple(where))
    return drawn.at[spots[0]].set(smallest).at[spots[1]].set(high)


def shard_levels(rng, shape, split, low, largest):
    def one(dim, blocks):
        steps = jax.random.uniform(jax.random.fold_in(jax.random.fold_in(rng, 6), dim), (blocks,), jnp.float32, low / len(split), largest / len(split))
        return jnp.repeat(jnp.exp(steps), shape[dim] // blocks).reshape((-1,) + (1,) * (len(shape) - dim - 1))

    gain = one(*split[0])
    for cut in split[1:]:
        gain = gain * one(*cut)
    return gain


def bell_draw(key, extent, scale, most, shards=(), dtype=jnp.bfloat16):
    result = scale * jax.random.normal(key, extent, jnp.float32)
    if shards:
        result = result * shard_levels(key, extent, shards, -0.22, 0.18)
    return jnp.clip(result, -most, most).astype(dtype)


def setup_inputs(seed: int = 0) -> dict:
    arg_keys = jax.random.split(jax.random.key(seed), 9)
    return {
        "vector": bell_draw(arg_keys[0], (NA, NB), 1.0, 6.0, ((0, 16), (1, 4)), jnp.float32),
        "op_alpha": draw_op_alpha(jax.random.fold_in(arg_keys[8], 71), 0),
        "op_beta": draw_op_beta(jax.random.fold_in(arg_keys[8], 71), 0),
        "op_weight": jnp.clip(jnp.exp(jax.random.uniform(arg_keys[3], (K,), jnp.float32, math.log(0.5), math.log(2.0))), 0.5, 2.0),
        "alpha_string": with_ends(jax.random.randint(arg_keys[4], (NA,), 0, STR), jax.random.fold_in(arg_keys[4], 1), 0, STR - 1).astype(jnp.int32),
        "beta_string": with_ends(jax.random.randint(arg_keys[5], (NB,), 0, STR), jax.random.fold_in(arg_keys[5], 1), 0, STR - 1).astype(jnp.int32),
        "alpha_energy": bell_draw(arg_keys[6], (STR,), 1.0, 4.0, (), jnp.float32),
        "beta_energy": bell_draw(arg_keys[7], (STR,), 1.0, 4.0, (), jnp.float32),
    }


def apply_operator(alpha_matrix, beta_matrix, block):
    highest = lax.Precision.HIGHEST
    left_part = jnp.dot(alpha_matrix, block, precision=highest, preferred_element_type=jnp.float32)
    right_part = jnp.dot(block, beta_matrix.T, precision=highest, preferred_element_type=jnp.float32)
    return left_part + right_part


def reference(vector, op_alpha, op_beta, op_weight, alpha_string, beta_string, alpha_energy, beta_energy):
    running = jnp.zeros(vector.shape, jnp.float32)
    for operator in range(K):
        inter = apply_operator(op_alpha[operator], op_beta[operator], vector)
        second = apply_operator(op_alpha[operator], op_beta[operator], inter)
        running = running + op_weight[operator] * second
    diag = alpha_energy[alpha_string][:, None] + beta_energy[beta_string][None, :]
    return diag * vector + 0.5 * running
```

```python
import jax
import jax.numpy as jnp
from jax import lax
from jax.sharding import PartitionSpec as P

AXES = ("alpha", "beta", "task")
NZ = 8
HIGH = lax.Precision.HIGH


def device_index(y_hi, z, y_lo, core, x):
    return ((y_hi * NZ + z) * 4 + y_lo * 2 + core) * 4 + x


def pairs(flip_hi=0, dz=0, flip_lo=0, flip_core=0, dx=0):
    table = []
    for y_hi in range(2):
        for z in range(NZ):
            for y_lo in range(2):
                for core in range(2):
                    for x in range(4):
                        here = device_index(y_hi, z, y_lo, core, x)
                        there = device_index(
                            y_hi ^ flip_hi, (z + dz) % NZ, y_lo ^ flip_lo, core ^ flip_core, (x + dx) % 4
                        )
                        table.append((here, there))
    return table


def move(block, **where):
    return lax.ppermute(block, AXES, pairs(**where))


def dot(left, right, left_dim, right_dim):
    return lax.dot_general(
        left, right, (((left_dim,), (right_dim,)), ((), ())),
        precision=HIGH, preferred_element_type=jnp.float32,
    )


def over_beta(block, beta):
    rows, width = block.shape
    core = move(block, flip_core=1)
    low = move(block, flip_lo=1)
    both = move(low, flip_core=1)
    whole = jnp.zeros((rows, 4 * width), block.dtype)
    for piece, at in ((block, beta), (core, beta ^ 1), (low, beta ^ 2), (both, beta ^ 3)):
        whole = lax.dynamic_update_slice_in_dim(whole, piece, at * width, 1)
    return whole


def on_device(
    vector, op_alpha, op_beta, op_weight, alpha_string, beta_string, alpha_energy, beta_energy
):
    rows, width = vector.shape
    quarter = width // 4
    half = NZ * rows
    alpha, beta, x = (lax.axis_index(name) for name in AXES)
    y_hi, z, core, odd = alpha // NZ, alpha % NZ, beta % 2, x % 2
    alpha_rows = op_alpha[0]
    beta_rows = op_beta[0]
    coefficient = 0.5 * op_weight[x]

    def columns(array, index):
        return lax.dynamic_slice_in_dim(array, index * quarter, quarter, 1)

    own_index = (odd, odd + 2)
    other_index = (1 - odd, 3 - odd)

    def gather(start, ups, x_step):
        held = {0: start}
        up = down = start
        passed = {}
        for step in range(1, 5):
            if step <= ups:
                up = move(up, dz=1)
                held[NZ - step] = up
                passed[NZ - step] = move(up, dx=x_step)
            if step <= 7 - ups:
                down = move(down, dz=-1)
                held[step] = down
                passed[step] = move(down, dx=x_step)
        return held, passed

    own_low, other_low = gather(columns(vector, own_index[0]), 4, 1)
    own_high, other_high = gather(columns(vector, own_index[1]), 3, -1)
    other_low[0] = columns(vector, other_index[0])
    other_high[0] = columns(vector, other_index[1])

    keep = lax.dynamic_slice_in_dim(alpha_rows, y_hi * half, half, 1)
    give = lax.dynamic_slice(alpha_rows, (core * (rows // 2), (1 - y_hi) * half), (rows // 2, half))
    got = move(give, flip_hi=1, flip_lo=1)
    got_core = move(got, flip_core=1)
    first = jnp.where(core == 0, got, got_core)
    second = jnp.where(core == 0, got_core, got)
    both = jnp.concatenate([keep, first, second], 0)
    operator = lax.dynamic_slice_in_dim(jnp.concatenate([both, both], 1), z * rows, half, 1)

    vector_beta = dot(over_beta(vector, beta), beta_rows, 1, 1)

    def inter_of(blocks, index):
        stacked = jnp.concatenate([blocks[d] for d in range(NZ)], 0)
        part = dot(operator, stacked, 1, 0)
        here = part[:rows] + columns(vector_beta, index)
        there = part[rows:]
        sent = move(jnp.concatenate([here, there], 0), flip_hi=1)
        return here + sent[rows:], there + sent[:rows]

    inter = [
        inter_of(own_low, own_index[0]),
        inter_of(other_low, other_index[0]),
        inter_of(own_high, own_index[1]),
        inter_of(other_high, other_index[1]),
    ]
    terms = [
        dot(operator, coefficient * jnp.concatenate(pair, 0), 0, 0) for pair in inter
    ]
    term_low, term_other_low, term_high, term_other_high = terms

    def natural(own_low, other_low, own_high, other_high):
        even = jnp.concatenate([own_low, other_low, own_high, other_high], 1)
        swapped = jnp.concatenate([other_low, own_low, other_high, own_high], 1)
        return jnp.where(odd == 0, even, swapped)

    inter_rows = natural(*[pair[0] for pair in inter])
    inter_beta = coefficient * dot(over_beta(inter_rows, beta), beta_rows, 1, 1)

    def scatter(term, term_other, ups, x_step, groups):
        summed = {}
        for low, high in groups:
            part = term[low * rows:high * rows] + move(term_other[low * rows:high * rows], dx=x_step)
            for d in range(low, high):
                summed[d] = part[(d - low) * rows:(d - low + 1) * rows]
        up = down = None
        for step in range(4, 0, -1):
            if step <= ups:
                up = summed[step] if up is None else summed[step] + up
                up = move(up, dz=1)
            if step <= 7 - ups:
                down = summed[NZ - step] if down is None else summed[NZ - step] + down
                down = move(down, dz=-1)
        return up + down

    arrived_low = scatter(term_low, term_other_low, 4, -1, ((3, 6), (6, 8), (1, 3)))
    arrived_high = scatter(term_high, term_other_high, 3, 1, ((3, 6), (1, 3), (6, 8)))

    own_rows = inter_beta + natural(
        term_low[:rows], term_other_low[:rows], term_high[:rows], term_other_high[:rows]
    )
    from_left = move(columns(own_rows, (x + 1) % 4), dx=1)
    from_right = move(columns(own_rows, (x + 3) % 4), dx=-1)
    first_pair = x < 2
    far = columns(own_rows, (x + 2) % 4) + jnp.where(first_pair, arrived_high, arrived_low)
    from_far = move(far, dx=2)
    total = columns(own_rows, x) + jnp.where(first_pair, arrived_low, arrived_high)
    total = total + from_left + from_right + from_far

    own_strings = lax.dynamic_slice_in_dim(beta_string, x * quarter, quarter, 0)
    diag = alpha_energy[alpha_string][:, None] + beta_energy[own_strings][None, :]
    return total + diag * columns(vector, x)


def solution(mesh):
    return jax.shard_map(
        on_device,
        mesh=mesh,
        in_specs=(
            P("alpha", "beta"),
            P("task", "alpha", None),
            P("task", "beta", None),
            P(),
            P("alpha"),
            P("beta"),
            P(),
            P(),
        ),
        out_specs=P("alpha", ("beta", "task")),
        check_vma=False,
    )
```

```python
import jax
import jax.numpy as jnp
from jax import lax
from jax.experimental import pallas as pl
from jax.experimental.pallas import tpu as pltpu
from jax.sharding import PartitionSpec as P

AXES = ("alpha", "beta", "task")
NZ = 8
HIGH = lax.Precision.HIGH


def device_index(y_hi, z, y_lo, core, x):
    return ((y_hi * NZ + z) * 4 + y_lo * 2 + core) * 4 + x


def pairs(flip_hi=0, dz=0, flip_lo=0, flip_core=0, dx=0):
    table = []
    for y_hi in range(2):
        for z in range(NZ):
            for y_lo in range(2):
                for core in range(2):
                    for x in range(4):
                        here = device_index(y_hi, z, y_lo, core, x)
                        there = device_index(
                            y_hi ^ flip_hi, (z + dz) % NZ, y_lo ^ flip_lo, core ^ flip_core, (x + dx) % 4
                        )
                        table.append((here, there))
    return table


def move(block, **where):
    return lax.ppermute(block, AXES, pairs(**where))


def dot(left, right, left_dim, right_dim):
    return lax.dot_general(
        left, right, (((left_dim,), (right_dim,)), ((), ())),
        precision=HIGH, preferred_element_type=jnp.float32,
    )


def together(*arrays):
    return lax.optimization_barrier(arrays)


def over_beta(block, beta):
    rows, width = block.shape
    core = move(block, flip_core=1)
    low = move(block, flip_lo=1)
    both = move(low, flip_core=1)
    whole = jnp.zeros((rows, 4 * width), block.dtype)
    for piece, at in ((block, beta), (core, beta ^ 1), (low, beta ^ 2), (both, beta ^ 3)):
        whole = lax.dynamic_update_slice_in_dim(whole, piece, at * width, 1)
    return whole


def split(value):
    high = value.astype(jnp.bfloat16)
    return high, (value - high.astype(jnp.float32)).astype(jnp.bfloat16)


def operator_kernel(place, own, taken, high, low):
    rows = own.shape[0]
    half = taken.shape[1]
    y_hi, z = place[0], place[1]
    for d in range(NZ):
        source = pl.multiple_of(lax.rem(z + d, NZ) * rows, rows)
        here = own[:, pl.ds(pl.multiple_of(y_hi * half + source, rows), rows)]
        there = taken[:, pl.ds(source, rows)]
        target = pl.ds(d * rows, rows)
        high[:rows, target], low[:rows, target] = split(here)
        high[rows:, target], low[rows:, target] = split(there)


def inter_kernel(op_high, op_low, beta_part, *refs):
    blocks, (out, high, low) = refs[:-3], refs[-3:]
    rows = beta_part.shape[0]
    at = 0
    for ref in blocks:
        size = ref.shape[0]
        high[at:at + size, :], low[at:at + size, :] = split(ref[...])
        at += size

    def product(left, right):
        return jnp.dot(left[...], right[...], preferred_element_type=jnp.float32)

    out[...] = product(op_high, high) + (product(op_high, low) + product(op_low, high))
    out[:rows, :] += beta_part[...]


def term_kernel(coefficient, op_high, op_low, own, sent, here, *refs):
    pieces, (high, low) = refs[:-2], refs[-2:]
    rows = own.shape[0] // 2
    upper = coefficient[0] * (own[:rows, :] + sent[rows:, :])
    lower = coefficient[0] * (own[rows:, :] + sent[:rows, :])
    here[...] = upper
    high[:rows, :], low[:rows, :] = split(upper)
    high[rows:, :], low[rows:, :] = split(lower)

    def product(left, right):
        return lax.dot_general(
            left, right, (((0,), (0,)), ((), ())), preferred_element_type=jnp.float32
        )

    at = 0
    for piece in pieces:
        span = slice(at, at + piece.shape[0])
        piece[...] = product(op_high[:, span], high[...]) + (
            product(op_high[:, span], low[...]) + product(op_low[:, span], high[...])
        )
        at += piece.shape[0]


VMEM = pl.BlockSpec(memory_space=pltpu.VMEM)
SMEM = pl.BlockSpec(memory_space=pltpu.SMEM)


def call(kernel, outputs, operands, specs, scratch, flops):
    moved = sum(a.size * a.dtype.itemsize for a in operands)
    moved += sum(o.size * o.dtype.itemsize for o in outputs)
    return pl.pallas_call(
        kernel,
        out_shape=outputs,
        in_specs=specs,
        out_specs=[VMEM] * len(outputs),
        scratch_shapes=scratch,
        compiler_params=pltpu.CompilerParams(vmem_limit_bytes=40 * 2**20),
        cost_estimate=pl.CostEstimate(flops=flops, bytes_accessed=moved, transcendentals=0),
    )(*operands)


def on_device(
    vector, op_alpha, op_beta, op_weight, alpha_string, beta_string, alpha_energy, beta_energy
):
    rows, width = vector.shape
    quarter = width // 4
    pair = 2 * quarter
    half = NZ * rows
    mid = rows // 2
    alpha, beta, x = (lax.axis_index(name) for name in AXES)
    y_hi, z, odd = alpha // NZ, alpha % NZ, x % 2
    alpha_rows = op_alpha[0]
    beta_rows = op_beta[0]
    coefficient = 0.5 * op_weight[x]

    def columns(array, index):
        return lax.dynamic_slice_in_dim(array, index * quarter, quarter, 1)

    def near_of(array):
        return jnp.concatenate([columns(array, odd), columns(array, odd + 2)], 1)

    def far_of(array):
        return jnp.concatenate([columns(array, 1 - odd), columns(array, 3 - odd)], 1)

    def natural(near, far):
        parts = [near[:, :quarter], far[:, :quarter], near[:, quarter:], far[:, quarter:]]
        even = jnp.concatenate(parts, 1)
        swapped = jnp.concatenate([parts[1], parts[0], parts[3], parts[2]], 1)
        return jnp.where(odd == 0, even, swapped)

    give = lax.dynamic_slice_in_dim(alpha_rows, (1 - y_hi) * half, half, 1)
    taken = move(give, flip_hi=1, flip_lo=1)

    start = near_of(vector)
    up1, down1 = move(start, dz=1), move(start, dz=-1)
    far_up1, far_down1 = move(up1, dx=-1), move(down1, dx=1)
    up2, down2 = move(up1, dz=1), move(down1, dz=-1)
    far_up2, far_down2 = move(up2, dx=-1), move(down2, dx=1)
    up3, down3 = move(up2, dz=1), move(down2, dz=-1)
    up3, down3, far_up1, far_down1 = together(up3, down3, far_up1, far_down1)
    far_up3, far_down3 = move(up3, dx=-1), move(down3, dx=1)
    up4, down4 = move(up3[:mid], dz=1), move(down3[mid:], dz=-1)
    up4, down4, far_up2, far_down2, taken = together(up4, down4, far_up2, far_down2, taken)
    far_up4, far_down4 = move(up4, dx=-1), move(down4, dx=1)
    near_blocks = [start, down1, down2, down3, up4, down4, up3, up2, up1]
    far_blocks = [
        far_of(vector), far_down1, far_down2, far_down3, far_up4, far_down4, far_up3, far_up2, far_up1
    ]

    place = jnp.stack([y_hi, z]).astype(jnp.int32)
    split_shape = jax.ShapeDtypeStruct((2 * rows, half), jnp.bfloat16)
    op_high, op_low = call(
        operator_kernel, [split_shape, split_shape], [place, alpha_rows, taken], [SMEM, VMEM, VMEM], [], 0
    )
    vector_beta = dot(lax.all_gather(vector, "beta", axis=1, tiled=True), beta_rows, 1, 1)

    def share_of(blocks, beta_part):
        operands = [op_high, op_low, beta_part, *blocks]
        return call(
            inter_kernel,
            [jax.ShapeDtypeStruct((2 * rows, pair), jnp.float32)],
            operands,
            [VMEM] * len(operands),
            [pltpu.VMEM((half, pair), jnp.bfloat16)] * 2,
            6 * 2 * rows * half * pair,
        )[0]

    def terms_of(share, sizes):
        sent = move(share, flip_hi=1)
        operands = [coefficient.reshape(1), op_high, op_low, share, sent]
        return call(
            term_kernel,
            [jax.ShapeDtypeStruct((size, pair), jnp.float32) for size in (rows, *sizes)],
            operands,
            [SMEM] + [VMEM] * 4,
            [pltpu.VMEM((2 * rows, pair), jnp.bfloat16)] * 2,
            6 * 2 * rows * half * pair,
        )

    sizes = (rows, 2 * rows, rows + mid, rows + mid, 2 * rows)
    near_share = share_of(near_blocks, near_of(vector_beta))
    far_share = share_of(far_blocks, far_of(vector_beta))
    near_here, near_own, near_12, near_34, near_45, near_67 = terms_of(near_share, sizes)
    upper = move(near_34, dx=1)
    lower = move(near_45, dx=-1)
    upper_rest = move(near_12, dx=1)
    lower_rest = move(near_67, dx=-1)
    far_here, far_own, far_12, far_34, far_45, far_67 = terms_of(far_share, sizes)

    inter_rows = natural(near_here, far_here)
    none = jnp.zeros((mid, pair), jnp.float32)
    up = move(far_34[rows:] + upper[rows:], dz=1)
    down = move(far_45[:mid] + lower[:mid], dz=-1)
    up, down = together(up, down)
    up = move(far_34[:rows] + upper[:rows] + jnp.concatenate([up, none], 0), dz=1)
    down = move(far_45[mid:] + lower[mid:] + jnp.concatenate([none, down], 0), dz=-1)
    up, down = together(up, down)
    up = move(far_12[rows:] + upper_rest[rows:] + up, dz=1)
    down = move(far_67[:rows] + lower_rest[:rows] + down, dz=-1)
    up, down = together(up, down)
    up = move(far_12[:rows] + upper_rest[:rows] + up, dz=1)
    down = move(far_67[rows:] + lower_rest[rows:] + down, dz=-1)
    arrived = up + down

    inter_beta = dot(over_beta(inter_rows, beta), beta_rows, 1, 1)
    own = inter_beta + natural(near_own, far_own)
    opposite = move(columns(own, (x + 2) % 4), dx=1)
    swap = (x == 1) | (x == 2)
    low, high = arrived[:, :quarter], arrived[:, quarter:]
    right = jnp.where(swap, high, low) + (columns(own, (x + 1) % 4) + opposite)
    left = jnp.where(swap, low, high) + columns(own, (x + 3) % 4)
    total = columns(own, x) + move(right, dx=1) + move(left, dx=-1)

    own_strings = lax.dynamic_slice_in_dim(beta_string, x * quarter, quarter, 0)
    diag = alpha_energy[alpha_string][:, None] + beta_energy[own_strings][None, :]
    return total + diag * columns(vector, x)


def solution(mesh):
    return jax.shard_map(
        on_device,
        mesh=mesh,
        in_specs=(
            P("alpha", "beta"),
            P("task", "alpha", None),
            P("task", "beta", None),
            P(),
            P("alpha"),
            P("beta"),
            P(),
            P(),
        ),
        out_specs=P("alpha", ("beta", "task")),
        check_vma=False,
    )
```

```python
import functools

import jax
import jax.numpy as jnp
from jax import lax
from jax.experimental import pallas as pl
from jax.experimental.pallas import tpu as pltpu
from jax.sharding import PartitionSpec as P

AXES = ("alpha", "beta", "task")
NZ = 8


def device_index(y_hi, z, y_lo, core, x):
    return ((y_hi * NZ + z) * 4 + y_lo * 2 + core) * 4 + x


def pairs(flip_hi=0, dz=0, flip_lo=0, flip_core=0, dx=0):
    table = []
    for y_hi in range(2):
        for z in range(NZ):
            for y_lo in range(2):
                for core in range(2):
                    for x in range(4):
                        here = device_index(y_hi, z, y_lo, core, x)
                        there = device_index(
                            y_hi ^ flip_hi, (z + dz) % NZ, y_lo ^ flip_lo, core ^ flip_core, (x + dx) % 4
                        )
                        table.append((here, there))
    return table


def move(block, **where):
    return lax.ppermute(block, AXES, pairs(**where))


def together(*arrays):
    return lax.optimization_barrier(arrays)


def split(value):
    high = value.astype(jnp.bfloat16)
    return high, (value - high.astype(jnp.float32)).astype(jnp.bfloat16)


def operator_kernel(place, own, taken, high, low):
    rows = own.shape[0]
    half = taken.shape[1]
    y_hi, z = place[0], place[1]
    for d in range(NZ):
        source = pl.multiple_of(lax.rem(z + d, NZ) * rows, rows)
        here = own[:, pl.ds(pl.multiple_of(y_hi * half + source, rows), rows)]
        there = taken[:, pl.ds(source, rows)]
        target = pl.ds(d * rows, rows)
        high[:rows, target], low[:rows, target] = split(here)
        high[rows:, target], low[rows:, target] = split(there)


def inter_kernel(op_high, op_low, beta_part, *refs):
    blocks, (out, high, low) = refs[:-3], refs[-3:]
    rows = beta_part.shape[0]
    at = 0
    for ref in blocks:
        size = ref.shape[0]
        high[at:at + size, :], low[at:at + size, :] = split(ref[...])
        at += size

    def product(left, right):
        return jnp.dot(left[...], right[...], preferred_element_type=jnp.float32)

    out[...] = product(op_high, high) + (product(op_high, low) + product(op_low, high))
    out[:rows, :] += beta_part[...]


def beta_kernel(columns, matrix, *refs):
    blocks, out = refs[:-1], refs[-1]
    width = out.shape[0] * 4
    total = jnp.zeros(out.shape, jnp.float32)
    for at, ref in enumerate(blocks):
        span = pl.ds(pl.multiple_of(columns[at], 256), width)
        left = ref[...] if ref.shape[1] == width else ref[:, span]
        left_high, left_low = split(left)
        right_high, right_low = split(matrix[:, span])

        def product(one, other):
            return lax.dot_general(
                one, other, (((1,), (1,)), ((), ())), preferred_element_type=jnp.float32
            )

        total += product(left_high, right_high) + (
            product(left_high, right_low) + product(left_low, right_high)
        )
    out[...] = total


def term_kernel(first, coefficient, op_high, op_low, own, sent, here, *refs):
    pieces, (high, low) = refs[:-2], refs[-2:]
    rows = own.shape[0] // 2
    upper = coefficient[0] * (own[:rows, :] + sent[rows:, :])
    lower = coefficient[0] * (own[rows:, :] + sent[:rows, :])
    here[...] = upper
    high[:rows, :], low[:rows, :] = split(upper)
    high[rows:, :], low[rows:, :] = split(lower)

    def product(left, right):
        return lax.dot_general(
            left, right, (((0,), (0,)), ((), ())), preferred_element_type=jnp.float32
        )

    at = first
    for piece in pieces:
        span = slice(at, at + piece.shape[0])
        piece[...] = product(op_high[:, span], high[...]) + (
            product(op_high[:, span], low[...]) + product(op_low[:, span], high[...])
        )
        at += piece.shape[0]


VMEM = pl.BlockSpec(memory_space=pltpu.VMEM)
SMEM = pl.BlockSpec(memory_space=pltpu.SMEM)


def call(kernel, outputs, operands, specs, scratch, flops):
    moved = sum(a.size * a.dtype.itemsize for a in operands)
    moved += sum(o.size * o.dtype.itemsize for o in outputs)
    return pl.pallas_call(
        kernel,
        out_shape=outputs,
        in_specs=specs,
        out_specs=[VMEM] * len(outputs),
        scratch_shapes=scratch,
        compiler_params=pltpu.CompilerParams(vmem_limit_bytes=24 * 2**20),
        cost_estimate=pl.CostEstimate(flops=flops, bytes_accessed=moved, transcendentals=0),
    )(*operands)


def beta_product(blocks, which, beta, matrix):
    rows = 256
    width = matrix.shape[0]
    columns = jnp.stack([(beta ^ one) * width for one in which]).astype(jnp.int32)
    moved = matrix.size * 4 + sum(block.size for block in blocks) * 4
    return pl.pallas_call(
        beta_kernel,
        grid=(width // rows,),
        out_shape=jax.ShapeDtypeStruct((rows, width), jnp.float32),
        in_specs=[SMEM, pl.BlockSpec((rows, matrix.shape[1]), lambda n: (n, 0))]
        + [pl.BlockSpec(block.shape, lambda n: (0, 0)) for block in blocks],
        out_specs=pl.BlockSpec((rows, rows), lambda n: (0, n)),
        compiler_params=pltpu.CompilerParams(vmem_limit_bytes=24 * 2**20),
        cost_estimate=pl.CostEstimate(
            flops=6 * rows * width * width * len(blocks), bytes_accessed=moved, transcendentals=0
        ),
    )(columns, matrix, *blocks)


def on_device(
    vector, op_alpha, op_beta, op_weight, alpha_string, beta_string, alpha_energy, beta_energy
):
    rows, width = vector.shape
    quarter = width // 4
    pair = 2 * quarter
    half = NZ * rows
    mid = rows // 2
    alpha, beta, x = (lax.axis_index(name) for name in AXES)
    y_hi, z, odd = alpha // NZ, alpha % NZ, x % 2
    alpha_rows = op_alpha[0]
    beta_rows = op_beta[0]
    coefficient = 0.5 * op_weight[x]

    def columns(array, index):
        return lax.dynamic_slice_in_dim(array, index * quarter, quarter, 1)

    def near_of(array):
        return jnp.concatenate([columns(array, odd), columns(array, odd + 2)], 1)

    def far_of(array):
        return jnp.concatenate([columns(array, 1 - odd), columns(array, 3 - odd)], 1)

    def natural(near, far):
        parts = [near[:, :quarter], far[:, :quarter], near[:, quarter:], far[:, quarter:]]
        even = jnp.concatenate(parts, 1)
        swapped = jnp.concatenate([parts[1], parts[0], parts[3], parts[2]], 1)
        return jnp.where(odd == 0, even, swapped)

    start = near_of(vector)
    start, other_half = together(start, (1 - y_hi) * half)
    give = lax.dynamic_slice_in_dim(alpha_rows, other_half, half, 1)
    taken = move(give, flip_hi=1, flip_lo=1)
    up1, down1 = move(start, dz=1), move(start, dz=-1)
    far_up1, far_down1 = move(up1, dx=-1), move(down1, dx=1)
    up2, down2 = move(up1, dz=1), move(down1, dz=-1)
    far_up2, far_down2 = move(up2, dx=-1), move(down2, dx=1)
    up3, down3 = move(up2, dz=1), move(down2, dz=-1)
    up3, down3, far_up1, far_down1 = together(up3, down3, far_up1, far_down1)
    far_up3, far_down3 = move(up3, dx=-1), move(down3, dx=1)
    up4, down4 = move(up3[:mid], dz=1), move(down3[mid:], dz=-1)
    up4, down4, far_up2, far_down2, taken = together(up4, down4, far_up2, far_down2, taken)
    far_up4, far_down4 = move(up4, dx=-1), move(down4, dx=1)
    place = jnp.stack([y_hi, z]).astype(jnp.int32)
    split_shape = jax.ShapeDtypeStruct((2 * rows, half), jnp.bfloat16)
    op_high, op_low = call(
        operator_kernel, [split_shape, split_shape], [place, alpha_rows, taken], [SMEM, VMEM, VMEM], [], 0
    )
    gathered = lax.all_gather(vector, "beta", axis=1, tiled=True)
    vector_beta = beta_product([vector], [0], beta, beta_rows) + beta_product(
        [gathered] * 3, [1, 2, 3], beta, beta_rows
    )

    def share_of(blocks, beta_part):
        operands = [op_high, op_low, beta_part, *blocks]
        return call(
            inter_kernel,
            [jax.ShapeDtypeStruct((2 * rows, pair), jnp.float32)],
            operands,
            [VMEM] * len(operands),
            [pltpu.VMEM((half, pair), jnp.bfloat16)] * 2,
            6 * 2 * rows * half * pair,
        )[0]

    def terms_of(share, sent, first, sizes):
        operands = [coefficient.reshape(1), op_high, op_low, share, sent]
        return call(
            functools.partial(term_kernel, first),
            [jax.ShapeDtypeStruct((size, pair), jnp.float32) for size in (rows, *sizes)],
            operands,
            [SMEM] + [VMEM] * 4,
            [pltpu.VMEM((2 * rows, pair), jnp.bfloat16)] * 2,
            6 * 2 * rows * sum(sizes) * pair,
        )

    near_beta, far_up3, far_down3, far_up4, far_down4 = together(
        near_of(vector_beta), far_up3, far_down3, far_up4, far_down4
    )
    near_blocks = [start, down1, down2, down3, up4, down4, up3, up2, up1]
    far_blocks = [
        far_of(vector), far_down1, far_down2, far_down3, far_up4, far_down4, far_up3, far_up2, far_up1
    ]
    near_share = share_of(near_blocks, near_beta)
    near_sent = move(near_share, flip_hi=1)
    far_share = share_of(far_blocks, far_of(vector_beta))
    far_sent = move(far_share, flip_hi=1)
    near_here, near_own, near_12, near_34, near_45, near_67 = terms_of(
        near_share, near_sent, 0, (rows, 2 * rows, rows + mid, rows + mid, 2 * rows)
    )
    upper = move(near_34, dx=1)
    lower = move(near_45, dx=-1)
    upper_rest = move(near_12, dx=1)
    lower_rest = move(near_67, dx=-1)
    far_here, far_34, far_45 = terms_of(far_share, far_sent, 3 * rows, (rows + mid, rows + mid))
    _, far_own, far_12 = terms_of(far_share, far_sent, 0, (rows, 2 * rows))
    _, far_67 = terms_of(far_share, far_sent, 6 * rows, (2 * rows,))

    none = jnp.zeros((mid, pair), jnp.float32)
    up = move(far_34[rows:] + upper[rows:], dz=1)
    down = move(far_45[:mid] + lower[:mid], dz=-1)
    up, down, far_here = together(up, down, far_here)
    inter_rows = natural(near_here, far_here)
    inter_core, inter_low = move(inter_rows, flip_core=1), move(inter_rows, flip_lo=1)
    up = move(far_34[:rows] + upper[:rows] + jnp.concatenate([up, none], 0), dz=1)
    down = move(far_45[mid:] + lower[mid:] + jnp.concatenate([none, down], 0), dz=-1)
    up, down = together(up, down)
    up = move(far_12[rows:] + upper_rest[rows:] + up, dz=1)
    down = move(far_67[:rows] + lower_rest[:rows] + down, dz=-1)
    up, down, inter_low, inter_core = together(up, down, inter_low, inter_core)
    inter_both = move(inter_low, flip_core=1)
    up = move(far_12[:rows] + upper_rest[:rows] + up, dz=1)
    down = move(far_67[rows:] + lower_rest[rows:] + down, dz=-1)
    arrived = up + down

    inter_beta = beta_product(
        [inter_rows, inter_core, inter_low, inter_both], [0, 1, 2, 3], beta, beta_rows
    )
    own = inter_beta + natural(near_own, far_own)
    opposite = move(columns(own, (x + 2) % 4), dx=1)
    swap = (x == 1) | (x == 2)
    low, high = arrived[:, :quarter], arrived[:, quarter:]
    right = jnp.where(swap, high, low) + (columns(own, (x + 1) % 4) + opposite)
    left = jnp.where(swap, low, high) + columns(own, (x + 3) % 4)
    total = columns(own, x) + move(right, dx=1) + move(left, dx=-1)

    own_strings = lax.dynamic_slice_in_dim(beta_string, x * quarter, quarter, 0)
    diag = alpha_energy[alpha_string][:, None] + beta_energy[own_strings][None, :]
    return total + diag * columns(vector, x)


def solution(mesh):
    return jax.shard_map(
        on_device,
        mesh=mesh,
        in_specs=(
            P("alpha", "beta"),
            P("task", "alpha", None),
            P("task", "beta", None),
            P(),
            P("alpha"),
            P("beta"),
            P(),
            P(),
        ),
        out_specs=P("alpha", ("beta", "task")),
        check_vma=False,
    )
```

```python
import jax
import jax.numpy as jnp
from jax import lax
from jax.experimental import pallas as pl
from jax.experimental.pallas import tpu as pltpu
from jax.sharding import PartitionSpec as P

AXES = ("alpha", "beta", "task")
NZ = 8
HIGH = lax.Precision.HIGH


def device_index(y_hi, z, y_lo, core, x):
    return ((y_hi * NZ + z) * 4 + y_lo * 2 + core) * 4 + x


def pairs(flip_hi=0, dz=0, flip_lo=0, flip_core=0, dx=0):
    table = []
    for y_hi in range(2):
        for z in range(NZ):
            for y_lo in range(2):
                for core in range(2):
                    for x in range(4):
                        here = device_index(y_hi, z, y_lo, core, x)
                        there = device_index(
                            y_hi ^ flip_hi, (z + dz) % NZ, y_lo ^ flip_lo, core ^ flip_core, (x + dx) % 4
                        )
                        table.append((here, there))
    return table


def move(block, **where):
    return lax.ppermute(block, AXES, pairs(**where))


def dot(left, right, left_dim, right_dim):
    return lax.dot_general(
        left, right, (((left_dim,), (right_dim,)), ((), ())),
        precision=HIGH, preferred_element_type=jnp.float32,
    )


def together(*arrays):
    return lax.optimization_barrier(arrays)


def side_by_side(beta, own, core, low, both):
    rows, width = own.shape
    whole = jnp.zeros((rows, 4 * width), own.dtype)
    for piece, at in ((own, beta), (core, beta ^ 1), (low, beta ^ 2), (both, beta ^ 3)):
        whole = lax.dynamic_update_slice_in_dim(whole, piece, at * width, 1)
    return whole


def split(value):
    high = value.astype(jnp.bfloat16)
    return high, (value - high.astype(jnp.float32)).astype(jnp.bfloat16)


def operator_kernel(place, own, taken, passed, high, low):
    rows = own.shape[0]
    half = taken.shape[1]
    mid = rows // 2
    y_hi, z, core = place[0], place[1], place[2]
    first = pl.ds(pl.multiple_of(rows + core * mid, mid), mid)
    second = pl.ds(pl.multiple_of(rows + (1 - core) * mid, mid), mid)
    for d in range(NZ):
        source = pl.multiple_of(lax.rem(z + d, NZ) * rows, rows)
        target = pl.ds(d * rows, rows)
        here = own[:, pl.ds(pl.multiple_of(y_hi * half + source, rows), rows)]
        high[:rows, target], low[:rows, target] = split(here)
        high[first, target], low[first, target] = split(taken[:, pl.ds(source, rows)])
        high[second, target], low[second, target] = split(passed[:, pl.ds(source, rows)])


def inter_kernel(op_high, op_low, beta_part, *refs):
    blocks, (out, high, low) = refs[:-3], refs[-3:]
    rows = beta_part.shape[0]
    at = 0
    for ref in blocks:
        size = ref.shape[0]
        high[at:at + size, :], low[at:at + size, :] = split(ref[...])
        at += size

    def product(left, right):
        return jnp.dot(left[...], right[...], preferred_element_type=jnp.float32)

    out[...] = product(op_high, high) + (product(op_high, low) + product(op_low, high))
    out[:rows, :] += beta_part[...]


def term_kernel(coefficient, op_high, op_low, own, sent, here, *refs):
    pieces, (high, low) = refs[:-2], refs[-2:]
    rows = own.shape[0] // 2
    upper = coefficient[0] * (own[:rows, :] + sent[rows:, :])
    lower = coefficient[0] * (own[rows:, :] + sent[:rows, :])
    here[...] = upper
    high[:rows, :], low[:rows, :] = split(upper)
    high[rows:, :], low[rows:, :] = split(lower)

    def product(left, right):
        return lax.dot_general(
            left, right, (((0,), (0,)), ((), ())), preferred_element_type=jnp.float32
        )

    at = 0
    for piece in pieces:
        span = slice(at, at + piece.shape[0])
        piece[...] = product(op_high[:, span], high[...]) + (
            product(op_high[:, span], low[...]) + product(op_low[:, span], high[...])
        )
        at += piece.shape[0]


VMEM = pl.BlockSpec(memory_space=pltpu.VMEM)
SMEM = pl.BlockSpec(memory_space=pltpu.SMEM)


def call(kernel, outputs, operands, specs, scratch, flops):
    moved = sum(a.size * a.dtype.itemsize for a in operands)
    moved += sum(o.size * o.dtype.itemsize for o in outputs)
    return pl.pallas_call(
        kernel,
        out_shape=outputs,
        in_specs=specs,
        out_specs=[VMEM] * len(outputs),
        scratch_shapes=scratch,
        compiler_params=pltpu.CompilerParams(vmem_limit_bytes=40 * 2**20),
        cost_estimate=pl.CostEstimate(flops=flops, bytes_accessed=moved, transcendentals=0),
    )(*operands)


def on_device(
    vector, op_alpha, op_beta, op_weight, alpha_string, beta_string, alpha_energy, beta_energy
):
    rows, width = vector.shape
    quarter = width // 4
    pair = 2 * quarter
    half = NZ * rows
    mid = rows // 2
    alpha, beta, x = (lax.axis_index(name) for name in AXES)
    y_hi, z, odd = alpha // NZ, alpha % NZ, x % 2
    alpha_rows = op_alpha[0]
    beta_rows = op_beta[0]
    coefficient = 0.5 * op_weight[x]

    def columns(array, index):
        return lax.dynamic_slice_in_dim(array, index * quarter, quarter, 1)

    def near_of(array):
        return jnp.concatenate([columns(array, odd), columns(array, odd + 2)], 1)

    def far_of(array):
        return jnp.concatenate([columns(array, 1 - odd), columns(array, 3 - odd)], 1)

    def natural(near, far):
        parts = [near[:, :quarter], far[:, :quarter], near[:, quarter:], far[:, quarter:]]
        even = jnp.concatenate(parts, 1)
        swapped = jnp.concatenate([parts[1], parts[0], parts[3], parts[2]], 1)
        return jnp.where(odd == 0, even, swapped)

    start = near_of(vector)
    up1, down1 = move(start, dz=1), move(start, dz=-1)
    core = beta % 2
    give = lax.dynamic_slice(alpha_rows, (core * mid, (1 - y_hi) * half), (mid, half))
    taken = move(give, flip_hi=1, flip_lo=1)
    passed = move(taken, flip_core=1)
    far_up1, far_down1 = move(up1, dx=-1), move(down1, dx=1)
    up2, down2 = move(up1, dz=1), move(down1, dz=-1)
    far_up2, far_down2 = move(up2, dx=-1), move(down2, dx=1)
    up3, down3 = move(up2, dz=1), move(down2, dz=-1)
    up3, down3, far_up1, far_down1 = together(up3, down3, far_up1, far_down1)
    far_up3, far_down3 = move(up3, dx=-1), move(down3, dx=1)
    up4, down4 = move(up3[:mid], dz=1), move(down3[mid:], dz=-1)
    vector_beta = dot(lax.all_gather(vector, "beta", axis=1, tiled=True), beta_rows, 1, 1)
    place = jnp.stack([y_hi, z, core]).astype(jnp.int32)
    up4, down4, far_up2, far_down2, far_up3, far_down3, vector_beta, place, passed = together(
        up4, down4, far_up2, far_down2, far_up3, far_down3, vector_beta, place, passed
    )
    far_up4, far_down4 = move(up4, dx=-1), move(down4, dx=1)
    near_blocks = [start, down1, down2, down3, up4, down4, up3, up2, up1]
    far_blocks = [
        far_of(vector), far_down1, far_down2, far_down3, far_up4, far_down4, far_up3, far_up2, far_up1
    ]

    split_shape = jax.ShapeDtypeStruct((2 * rows, half), jnp.bfloat16)
    op_high, op_low = call(
        operator_kernel, [split_shape, split_shape], [place, alpha_rows, taken, passed], [SMEM, VMEM, VMEM, VMEM], [], 0
    )

    def share_of(blocks, beta_part):
        operands = [op_high, op_low, beta_part, *blocks]
        return call(
            inter_kernel,
            [jax.ShapeDtypeStruct((2 * rows, pair), jnp.float32)],
            operands,
            [VMEM] * len(operands),
            [pltpu.VMEM((half, pair), jnp.bfloat16)] * 2,
            6 * 2 * rows * half * pair,
        )[0]

    def terms_of(share, sizes):
        sent = move(share, flip_hi=1)
        operands = [coefficient.reshape(1), op_high, op_low, share, sent]
        return call(
            term_kernel,
            [jax.ShapeDtypeStruct((size, pair), jnp.float32) for size in (rows, *sizes)],
            operands,
            [SMEM] + [VMEM] * 4,
            [pltpu.VMEM((2 * rows, pair), jnp.bfloat16)] * 2,
            6 * 2 * rows * half * pair,
        )

    sizes = (rows, 2 * rows, rows + mid, rows + mid, 2 * rows)
    near_share = share_of(near_blocks, near_of(vector_beta))
    far_share = share_of(far_blocks, far_of(vector_beta))
    near_here, near_own, near_12, near_34, near_45, near_67 = terms_of(near_share, sizes)
    upper = move(near_34, dx=1)
    lower = move(near_45, dx=-1)
    upper_rest = move(near_12, dx=1)
    lower_rest = move(near_67, dx=-1)
    far_here, far_own, far_12, far_34, far_45, far_67 = terms_of(far_share, sizes)

    inter_rows = natural(near_here, far_here)
    inter_core, inter_low = move(inter_rows, flip_core=1), move(inter_rows, flip_lo=1)
    none = jnp.zeros((mid, pair), jnp.float32)
    up = move(far_34[rows:] + upper[rows:], dz=1)
    down = move(far_45[:mid] + lower[:mid], dz=-1)
    up, down = together(up, down)
    up = move(far_34[:rows] + upper[:rows] + jnp.concatenate([up, none], 0), dz=1)
    down = move(far_45[mid:] + lower[mid:] + jnp.concatenate([none, down], 0), dz=-1)
    up, down, inter_low = together(up, down, inter_low)
    inter_both = move(inter_low, flip_core=1)
    up = move(far_12[rows:] + upper_rest[rows:] + up, dz=1)
    down = move(far_67[:rows] + lower_rest[:rows] + down, dz=-1)
    up, down = together(up, down)
    up = move(far_12[:rows] + upper_rest[:rows] + up, dz=1)
    down = move(far_67[rows:] + lower_rest[rows:] + down, dz=-1)
    arrived = up + down

    inter_beta = dot(
        side_by_side(beta, inter_rows, inter_core, inter_low, inter_both), beta_rows, 1, 1
    )
    own = inter_beta + natural(near_own, far_own)
    opposite = move(columns(own, (x + 2) % 4), dx=2)
    swap = (x == 1) | (x == 2)
    low, high = arrived[:, :quarter], arrived[:, quarter:]
    right = jnp.where(swap, high, low) + columns(own, (x + 1) % 4)
    left = jnp.where(swap, low, high) + columns(own, (x + 3) % 4)
    total = columns(own, x) + move(right, dx=1) + move(left, dx=-1) + opposite

    own_strings = lax.dynamic_slice_in_dim(beta_string, x * quarter, quarter, 0)
    diag = alpha_energy[alpha_string][:, None] + beta_energy[own_strings][None, :]
    return total + diag * columns(vector, x)


def solution(mesh):
    return jax.shard_map(
        on_device,
        mesh=mesh,
        in_specs=(
            P("alpha", "beta"),
            P("task", "alpha", None),
            P("task", "beta", None),
            P(),
            P("alpha"),
            P("beta"),
            P(),
            P(),
        ),
        out_specs=P("alpha", ("beta", "task")),
        check_vma=False,
    )
```

```python
import jax
import jax.numpy as jnp
from jax import lax
from jax.experimental import pallas as pl
from jax.experimental.pallas import tpu as pltpu
from jax.sharding import PartitionSpec as P

AXES = ("alpha", "beta", "task")
NZ = 8
HIGH = lax.Precision.HIGH


def device_index(y_hi, z, y_lo, core, x):
    return ((y_hi * NZ + z) * 4 + y_lo * 2 + core) * 4 + x


def pairs(flip_hi=0, dz=0, flip_lo=0, flip_core=0, dx=0):
    table = []
    for y_hi in range(2):
        for z in range(NZ):
            for y_lo in range(2):
                for core in range(2):
                    for x in range(4):
                        here = device_index(y_hi, z, y_lo, core, x)
                        there = device_index(
                            y_hi ^ flip_hi, (z + dz) % NZ, y_lo ^ flip_lo, core ^ flip_core, (x + dx) % 4
                        )
                        table.append((here, there))
    return table


def move(block, **where):
    return lax.ppermute(block, AXES, pairs(**where))


def dot(left, right, left_dim, right_dim):
    return lax.dot_general(
        left, right, (((left_dim,), (right_dim,)), ((), ())),
        precision=HIGH, preferred_element_type=jnp.float32,
    )


def together(*arrays):
    return lax.optimization_barrier(arrays)


def side_by_side(beta, own, core, low, both):
    rows, width = own.shape
    whole = jnp.zeros((rows, 4 * width), own.dtype)
    for piece, at in ((own, beta), (core, beta ^ 1), (low, beta ^ 2), (both, beta ^ 3)):
        whole = lax.dynamic_update_slice_in_dim(whole, piece, at * width, 1)
    return whole


def split(value):
    high = value.astype(jnp.bfloat16)
    return high, (value - high.astype(jnp.float32)).astype(jnp.bfloat16)


def operator_kernel(place, own, taken, passed, high, low):
    rows = own.shape[0]
    half = taken.shape[1]
    mid = rows // 2
    y_hi, z, core = place[0], place[1], place[2]
    first = pl.ds(pl.multiple_of(rows + core * mid, mid), mid)
    second = pl.ds(pl.multiple_of(rows + (1 - core) * mid, mid), mid)
    for d in range(NZ):
        source = pl.multiple_of(lax.rem(z + d, NZ) * rows, rows)
        target = pl.ds(d * rows, rows)
        here = own[:, pl.ds(pl.multiple_of(y_hi * half + source, rows), rows)]
        high[:rows, target], low[:rows, target] = split(here)
        high[first, target], low[first, target] = split(taken[:, pl.ds(source, rows)])
        high[second, target], low[second, target] = split(passed[:, pl.ds(source, rows)])


def inter_kernel(op_high, op_low, beta_part, *refs):
    blocks, (out, high, low) = refs[:-3], refs[-3:]
    rows = beta_part.shape[0]
    at = 0
    for ref in blocks:
        size = ref.shape[0]
        high[at:at + size, :], low[at:at + size, :] = split(ref[...])
        at += size

    def product(left, right):
        return jnp.dot(left[...], right[...], preferred_element_type=jnp.float32)

    out[...] = product(op_high, high) + (product(op_high, low) + product(op_low, high))
    out[:rows, :] += beta_part[...]


def term_kernel(coefficient, op_high, op_low, own, sent, here, *refs):
    pieces, (high, low) = refs[:-2], refs[-2:]
    rows = own.shape[0] // 2
    upper = coefficient[0] * (own[:rows, :] + sent[rows:, :])
    lower = coefficient[0] * (own[rows:, :] + sent[:rows, :])
    here[...] = upper
    high[:rows, :], low[:rows, :] = split(upper)
    high[rows:, :], low[rows:, :] = split(lower)

    def product(left, right):
        return lax.dot_general(
            left, right, (((0,), (0,)), ((), ())), preferred_element_type=jnp.float32
        )

    at = 0
    for piece in pieces:
        span = slice(at, at + piece.shape[0])
        piece[...] = product(op_high[:, span], high[...]) + (
            product(op_high[:, span], low[...]) + product(op_low[:, span], high[...])
        )
        at += piece.shape[0]


VMEM = pl.BlockSpec(memory_space=pltpu.VMEM)
SMEM = pl.BlockSpec(memory_space=pltpu.SMEM)


def call(kernel, outputs, operands, specs, scratch, flops):
    moved = sum(a.size * a.dtype.itemsize for a in operands)
    moved += sum(o.size * o.dtype.itemsize for o in outputs)
    return pl.pallas_call(
        kernel,
        out_shape=outputs,
        in_specs=specs,
        out_specs=[VMEM] * len(outputs),
        scratch_shapes=scratch,
        compiler_params=pltpu.CompilerParams(vmem_limit_bytes=40 * 2**20),
        cost_estimate=pl.CostEstimate(flops=flops, bytes_accessed=moved, transcendentals=0),
    )(*operands)


def on_device(
    vector, op_alpha, op_beta, op_weight, alpha_string, beta_string, alpha_energy, beta_energy
):
    rows, width = vector.shape
    quarter = width // 4
    pair = 2 * quarter
    half = NZ * rows
    mid = rows // 2
    alpha, beta, x = (lax.axis_index(name) for name in AXES)
    y_hi, z, odd = alpha // NZ, alpha % NZ, x % 2
    alpha_rows = op_alpha[0]
    beta_rows = op_beta[0]
    coefficient = 0.5 * op_weight[x]

    def columns(array, index):
        return lax.dynamic_slice_in_dim(array, index * quarter, quarter, 1)

    def near_of(array):
        return jnp.concatenate([columns(array, odd), columns(array, odd + 2)], 1)

    def far_of(array):
        return jnp.concatenate([columns(array, 1 - odd), columns(array, 3 - odd)], 1)

    def natural(near, far):
        parts = [near[:, :quarter], far[:, :quarter], near[:, quarter:], far[:, quarter:]]
        even = jnp.concatenate(parts, 1)
        swapped = jnp.concatenate([parts[1], parts[0], parts[3], parts[2]], 1)
        return jnp.where(odd == 0, even, swapped)

    start = near_of(vector)
    up1, down1 = move(start, dz=1), move(start, dz=-1)
    core = beta % 2
    give = lax.dynamic_slice(alpha_rows, (core * mid, (1 - y_hi) * half), (mid, half))
    taken = move(give, flip_hi=1, flip_lo=1)
    passed = move(taken, flip_core=1)
    beta_low, beta_core = move(vector, flip_lo=1), move(vector, flip_core=1)
    far_up1, far_down1 = move(up1, dx=-1), move(down1, dx=1)
    up2, down2 = move(up1, dz=1), move(down1, dz=-1)
    up2, down2, beta_low = together(up2, down2, beta_low)
    beta_both = move(beta_low, flip_core=1)
    far_up2, far_down2 = move(up2, dx=-1), move(down2, dx=1)
    up3, down3 = move(up2, dz=1), move(down2, dz=-1)
    up3, down3, far_up1, far_down1 = together(up3, down3, far_up1, far_down1)
    far_up3, far_down3 = move(up3, dx=-1), move(down3, dx=1)
    up4, down4 = move(up3[:mid], dz=1), move(down3[mid:], dz=-1)
    vector_beta = dot(
        side_by_side(beta, vector, beta_core, beta_low, beta_both), beta_rows, 1, 1
    )
    place = jnp.stack([y_hi, z, core]).astype(jnp.int32)
    up4, down4, far_up2, far_down2, far_up3, far_down3, vector_beta, place, passed = together(
        up4, down4, far_up2, far_down2, far_up3, far_down3, vector_beta, place, passed
    )
    far_up4, far_down4 = move(up4, dx=-1), move(down4, dx=1)
    near_blocks = [start, down1, down2, down3, up4, down4, up3, up2, up1]
    far_blocks = [
        far_of(vector), far_down1, far_down2, far_down3, far_up4, far_down4, far_up3, far_up2, far_up1
    ]

    split_shape = jax.ShapeDtypeStruct((2 * rows, half), jnp.bfloat16)
    op_high, op_low = call(
        operator_kernel, [split_shape, split_shape], [place, alpha_rows, taken, passed], [SMEM, VMEM, VMEM, VMEM], [], 0
    )

    def share_of(blocks, beta_part):
        operands = [op_high, op_low, beta_part, *blocks]
        return call(
            inter_kernel,
            [jax.ShapeDtypeStruct((2 * rows, pair), jnp.float32)],
            operands,
            [VMEM] * len(operands),
            [pltpu.VMEM((half, pair), jnp.bfloat16)] * 2,
            6 * 2 * rows * half * pair,
        )[0]

    def terms_of(share, sizes):
        sent = move(share, flip_hi=1)
        operands = [coefficient.reshape(1), op_high, op_low, share, sent]
        return call(
            term_kernel,
            [jax.ShapeDtypeStruct((size, pair), jnp.float32) for size in (rows, *sizes)],
            operands,
            [SMEM] + [VMEM] * 4,
            [pltpu.VMEM((2 * rows, pair), jnp.bfloat16)] * 2,
            6 * 2 * rows * half * pair,
        )

    sizes = (rows, 2 * rows, rows + mid, rows + mid, 2 * rows)
    near_share = share_of(near_blocks, near_of(vector_beta))
    far_share = share_of(far_blocks, far_of(vector_beta))
    near_here, near_own, near_12, near_34, near_45, near_67 = terms_of(near_share, sizes)
    upper = move(near_34, dx=1)
    lower = move(near_45, dx=-1)
    upper_rest = move(near_12, dx=1)
    lower_rest = move(near_67, dx=-1)
    far_here, far_own, far_12, far_34, far_45, far_67 = terms_of(far_share, sizes)

    inter_rows = natural(near_here, far_here)
    inter_core, inter_low = move(inter_rows, flip_core=1), move(inter_rows, flip_lo=1)
    none = jnp.zeros((mid, pair), jnp.float32)
    up = move(far_34[rows:] + upper[rows:], dz=1)
    down = move(far_45[:mid] + lower[:mid], dz=-1)
    up, down = together(up, down)
    up = move(far_34[:rows] + upper[:rows] + jnp.concatenate([up, none], 0), dz=1)
    down = move(far_45[mid:] + lower[mid:] + jnp.concatenate([none, down], 0), dz=-1)
    up, down, inter_low = together(up, down, inter_low)
    inter_both = move(inter_low, flip_core=1)
    up = move(far_12[rows:] + upper_rest[rows:] + up, dz=1)
    down = move(far_67[:rows] + lower_rest[:rows] + down, dz=-1)
    up, down = together(up, down)
    up = move(far_12[:rows] + upper_rest[:rows] + up, dz=1)
    down = move(far_67[rows:] + lower_rest[rows:] + down, dz=-1)
    arrived = up + down

    inter_beta = dot(
        side_by_side(beta, inter_rows, inter_core, inter_low, inter_both), beta_rows, 1, 1
    )
    own = inter_beta + natural(near_own, far_own)
    opposite = move(columns(own, (x + 2) % 4), dx=2)
    swap = (x == 1) | (x == 2)
    low, high = arrived[:, :quarter], arrived[:, quarter:]
    right = jnp.where(swap, high, low) + columns(own, (x + 1) % 4)
    left = jnp.where(swap, low, high) + columns(own, (x + 3) % 4)
    total = columns(own, x) + move(right, dx=1) + move(left, dx=-1) + opposite

    own_strings = lax.dynamic_slice_in_dim(beta_string, x * quarter, quarter, 0)
    diag = alpha_energy[alpha_string][:, None] + beta_energy[own_strings][None, :]
    return total + diag * columns(vector, x)


def solution(mesh):
    return jax.shard_map(
        on_device,
        mesh=mesh,
        in_specs=(
            P("alpha", "beta"),
            P("task", "alpha", None),
            P("task", "beta", None),
            P(),
            P("alpha"),
            P("beta"),
            P(),
            P(),
        ),
        out_specs=P("alpha", ("beta", "task")),
        check_vma=False,
    )
```

```python
import jax
import jax.numpy as jnp
from jax import lax
from jax.experimental import pallas as pl
from jax.experimental.pallas import tpu as pltpu
from jax.sharding import PartitionSpec as P

AXES = ("alpha", "beta", "task")
NZ = 8
HIGH = lax.Precision.HIGH


def device_index(y_hi, z, y_lo, core, x):
    return ((y_hi * NZ + z) * 4 + y_lo * 2 + core) * 4 + x


def pairs(flip_hi=0, dz=0, flip_lo=0, flip_core=0, dx=0):
    table = []
    for y_hi in range(2):
        for z in range(NZ):
            for y_lo in range(2):
                for core in range(2):
                    for x in range(4):
                        here = device_index(y_hi, z, y_lo, core, x)
                        there = device_index(
                            y_hi ^ flip_hi, (z + dz) % NZ, y_lo ^ flip_lo, core ^ flip_core, (x + dx) % 4
                        )
                        table.append((here, there))
    return table


def move(block, **where):
    return lax.ppermute(block, AXES, pairs(**where))


def dot(left, right, left_dim, right_dim):
    return lax.dot_general(
        left, right, (((left_dim,), (right_dim,)), ((), ())),
        precision=HIGH, preferred_element_type=jnp.float32,
    )


def together(*arrays):
    return lax.optimization_barrier(arrays)


def side_by_side(beta, own, core, low, both):
    rows, width = own.shape
    whole = jnp.zeros((rows, 4 * width), own.dtype)
    for piece, at in ((own, beta), (core, beta ^ 1), (low, beta ^ 2), (both, beta ^ 3)):
        whole = lax.dynamic_update_slice_in_dim(whole, piece, at * width, 1)
    return whole


def split(value):
    high = value.astype(jnp.bfloat16)
    return high, (value - high.astype(jnp.float32)).astype(jnp.bfloat16)


def operator_kernel(place, own, taken, passed, high, low):
    rows = own.shape[0]
    half = taken.shape[1]
    mid = rows // 2
    y_hi, z, core = place[0], place[1], place[2]
    first = pl.ds(pl.multiple_of(rows + core * mid, mid), mid)
    second = pl.ds(pl.multiple_of(rows + (1 - core) * mid, mid), mid)
    for d in range(NZ):
        source = pl.multiple_of(lax.rem(z + d, NZ) * rows, rows)
        target = pl.ds(d * rows, rows)
        here = own[:, pl.ds(pl.multiple_of(y_hi * half + source, rows), rows)]
        high[:rows, target], low[:rows, target] = split(here)
        high[first, target], low[first, target] = split(taken[:, pl.ds(source, rows)])
        high[second, target], low[second, target] = split(passed[:, pl.ds(source, rows)])


def inter_kernel(op_high, op_low, beta_part, *refs):
    blocks, (out, high, low) = refs[:-3], refs[-3:]
    rows = beta_part.shape[0]
    at = 0
    for ref in blocks:
        size = ref.shape[0]
        high[at:at + size, :], low[at:at + size, :] = split(ref[...])
        at += size

    def product(left, right):
        return jnp.dot(left[...], right[...], preferred_element_type=jnp.float32)

    out[...] = product(op_high, high) + (product(op_high, low) + product(op_low, high))
    out[:rows, :] += beta_part[...]


def term_kernel(coefficient, op_high, op_low, own, sent, here, *refs):
    pieces, (high, low) = refs[:-2], refs[-2:]
    rows = own.shape[0] // 2
    upper = coefficient[0] * (own[:rows, :] + sent[rows:, :])
    lower = coefficient[0] * (own[rows:, :] + sent[:rows, :])
    here[...] = upper
    high[:rows, :], low[:rows, :] = split(upper)
    high[rows:, :], low[rows:, :] = split(lower)

    def product(left, right):
        return lax.dot_general(
            left, right, (((0,), (0,)), ((), ())), preferred_element_type=jnp.float32
        )

    at = 0
    for piece in pieces:
        span = slice(at, at + piece.shape[0])
        piece[...] = product(op_high[:, span], high[...]) + (
            product(op_high[:, span], low[...]) + product(op_low[:, span], high[...])
        )
        at += piece.shape[0]


VMEM = pl.BlockSpec(memory_space=pltpu.VMEM)
SMEM = pl.BlockSpec(memory_space=pltpu.SMEM)


def call(kernel, outputs, operands, specs, scratch, flops):
    moved = sum(a.size * a.dtype.itemsize for a in operands)
    moved += sum(o.size * o.dtype.itemsize for o in outputs)
    return pl.pallas_call(
        kernel,
        out_shape=outputs,
        in_specs=specs,
        out_specs=[VMEM] * len(outputs),
        scratch_shapes=scratch,
        compiler_params=pltpu.CompilerParams(vmem_limit_bytes=40 * 2**20),
        cost_estimate=pl.CostEstimate(flops=flops, bytes_accessed=moved, transcendentals=0),
    )(*operands)


def on_device(
    vector, op_alpha, op_beta, op_weight, alpha_string, beta_string, alpha_energy, beta_energy
):
    rows, width = vector.shape
    quarter = width // 4
    pair = 2 * quarter
    half = NZ * rows
    mid = rows // 2
    alpha, beta, x = (lax.axis_index(name) for name in AXES)
    y_hi, z, odd = alpha // NZ, alpha % NZ, x % 2
    alpha_rows = op_alpha[0]
    beta_rows = op_beta[0]
    coefficient = 0.5 * op_weight[x]

    def columns(array, index):
        return lax.dynamic_slice_in_dim(array, index * quarter, quarter, 1)

    def near_of(array):
        return jnp.concatenate([columns(array, odd), columns(array, odd + 2)], 1)

    def far_of(array):
        return jnp.concatenate([columns(array, 1 - odd), columns(array, 3 - odd)], 1)

    def natural(near, far):
        parts = [near[:, :quarter], far[:, :quarter], near[:, quarter:], far[:, quarter:]]
        even = jnp.concatenate(parts, 1)
        swapped = jnp.concatenate([parts[1], parts[0], parts[3], parts[2]], 1)
        return jnp.where(odd == 0, even, swapped)

    start = near_of(vector)
    up1, down1 = move(start, dz=1), move(start, dz=-1)
    core = beta % 2
    give = lax.dynamic_slice(alpha_rows, (core * mid, (1 - y_hi) * half), (mid, half))
    taken = move(give, flip_hi=1, flip_lo=1)
    passed = move(taken, flip_core=1)
    beta_low, beta_core = move(vector, flip_lo=1), move(vector, flip_core=1)
    far_up1, far_down1 = move(up1, dx=-1), move(down1, dx=1)
    up2, down2 = move(up1, dz=1), move(down1, dz=-1)
    far_up2, far_down2 = move(up2, dx=-1), move(down2, dx=1)
    up3, down3 = move(up2, dz=1), move(down2, dz=-1)
    up3, down3, far_up1, far_down1, beta_low = together(up3, down3, far_up1, far_down1, beta_low)
    beta_both = move(beta_low, flip_core=1)
    far_up3, far_down3 = move(up3, dx=-1), move(down3, dx=1)
    up4, down4 = move(up3[:mid], dz=1), move(down3[mid:], dz=-1)
    vector_beta = dot(
        side_by_side(beta, vector, beta_core, beta_low, beta_both), beta_rows, 1, 1
    )
    place = jnp.stack([y_hi, z, core]).astype(jnp.int32)
    up4, down4, far_up2, far_down2, far_up3, far_down3, vector_beta, place, passed = together(
        up4, down4, far_up2, far_down2, far_up3, far_down3, vector_beta, place, passed
    )
    far_up4, far_down4 = move(up4, dx=-1), move(down4, dx=1)
    near_blocks = [start, down1, down2, down3, up4, down4, up3, up2, up1]
    far_blocks = [
        far_of(vector), far_down1, far_down2, far_down3, far_up4, far_down4, far_up3, far_up2, far_up1
    ]

    split_shape = jax.ShapeDtypeStruct((2 * rows, half), jnp.bfloat16)
    op_high, op_low = call(
        operator_kernel, [split_shape, split_shape], [place, alpha_rows, taken, passed], [SMEM, VMEM, VMEM, VMEM], [], 0
    )

    def share_of(blocks, beta_part):
        operands = [op_high, op_low, beta_part, *blocks]
        return call(
            inter_kernel,
            [jax.ShapeDtypeStruct((2 * rows, pair), jnp.float32)],
            operands,
            [VMEM] * len(operands),
            [pltpu.VMEM((half, pair), jnp.bfloat16)] * 2,
            6 * 2 * rows * half * pair,
        )[0]

    def terms_of(share, sizes):
        sent = move(share, flip_hi=1)
        operands = [coefficient.reshape(1), op_high, op_low, share, sent]
        return call(
            term_kernel,
            [jax.ShapeDtypeStruct((size, pair), jnp.float32) for size in (rows, *sizes)],
            operands,
            [SMEM] + [VMEM] * 4,
            [pltpu.VMEM((2 * rows, pair), jnp.bfloat16)] * 2,
            6 * 2 * rows * half * pair,
        )

    sizes = (rows, 2 * rows, rows + mid, rows + mid, 2 * rows)
    near_share = share_of(near_blocks, near_of(vector_beta))
    far_share = share_of(far_blocks, far_of(vector_beta))
    near_here, near_own, near_12, near_34, near_45, near_67 = terms_of(near_share, sizes)
    upper = move(near_34, dx=1)
    lower = move(near_45, dx=-1)
    upper_rest = move(near_12, dx=1)
    lower_rest = move(near_67, dx=-1)
    far_here, far_own, far_12, far_34, far_45, far_67 = terms_of(far_share, sizes)

    inter_rows = natural(near_here, far_here)
    inter_core, inter_low = move(inter_rows, flip_core=1), move(inter_rows, flip_lo=1)
    none = jnp.zeros((mid, pair), jnp.float32)
    up = move(far_34[rows:] + upper[rows:], dz=1)
    down = move(far_45[:mid] + lower[:mid], dz=-1)
    up, down = together(up, down)
    up = move(far_34[:rows] + upper[:rows] + jnp.concatenate([up, none], 0), dz=1)
    down = move(far_45[mid:] + lower[mid:] + jnp.concatenate([none, down], 0), dz=-1)
    up, down, inter_low = together(up, down, inter_low)
    inter_both = move(inter_low, flip_core=1)
    up = move(far_12[rows:] + upper_rest[rows:] + up, dz=1)
    down = move(far_67[:rows] + lower_rest[:rows] + down, dz=-1)
    inter_whole = side_by_side(beta, inter_rows, inter_core, inter_low, inter_both)
    up, down, inter_whole = together(up, down, inter_whole)
    up = move(far_12[:rows] + upper_rest[:rows] + up, dz=1)
    down = move(far_67[rows:] + lower_rest[rows:] + down, dz=-1)
    arrived = up + down

    inter_beta = dot(inter_whole, beta_rows, 1, 1)
    own = inter_beta + natural(near_own, far_own)
    opposite = move(columns(own, (x + 2) % 4), dx=2)
    swap = (x == 1) | (x == 2)
    low, high = arrived[:, :quarter], arrived[:, quarter:]
    right = jnp.where(swap, high, low) + columns(own, (x + 1) % 4)
    left = jnp.where(swap, low, high) + columns(own, (x + 3) % 4)
    total = columns(own, x) + move(right, dx=1) + move(left, dx=-1) + opposite

    own_strings = lax.dynamic_slice_in_dim(beta_string, x * quarter, quarter, 0)
    diag = alpha_energy[alpha_string][:, None] + beta_energy[own_strings][None, :]
    return total + diag * columns(vector, x)


def solution(mesh):
    return jax.shard_map(
        on_device,
        mesh=mesh,
        in_specs=(
            P("alpha", "beta"),
            P("task", "alpha", None),
            P("task", "beta", None),
            P(),
            P("alpha"),
            P("beta"),
            P(),
            P(),
        ),
        out_specs=P("alpha", ("beta", "task")),
        check_vma=False,
    )
```

```python
import jax
import jax.numpy as jnp
from jax import lax
from jax.experimental import pallas as pl
from jax.experimental.pallas import tpu as pltpu
from jax.sharding import PartitionSpec as P

AXES = ("alpha", "beta", "task")
NZ = 8
HIGH = lax.Precision.HIGH


def device_index(y_hi, z, y_lo, core, x):
    return ((y_hi * NZ + z) * 4 + y_lo * 2 + core) * 4 + x


def pairs(flip_hi=0, dz=0, flip_lo=0, flip_core=0, dx=0):
    table = []
    for y_hi in range(2):
        for z in range(NZ):
            for y_lo in range(2):
                for core in range(2):
                    for x in range(4):
                        here = device_index(y_hi, z, y_lo, core, x)
                        there = device_index(
                            y_hi ^ flip_hi, (z + dz) % NZ, y_lo ^ flip_lo, core ^ flip_core, (x + dx) % 4
                        )
                        table.append((here, there))
    return table


def move(block, **where):
    return lax.ppermute(block, AXES, pairs(**where))


def dot(left, right, left_dim, right_dim):
    return lax.dot_general(
        left, right, (((left_dim,), (right_dim,)), ((), ())),
        precision=HIGH, preferred_element_type=jnp.float32,
    )


def together(*arrays):
    return lax.optimization_barrier(arrays)


def side_by_side(beta, own, core, low, both):
    rows, width = own.shape
    whole = jnp.zeros((rows, 4 * width), own.dtype)
    for piece, at in ((own, beta), (core, beta ^ 1), (low, beta ^ 2), (both, beta ^ 3)):
        whole = lax.dynamic_update_slice_in_dim(whole, piece, at * width, 1)
    return whole


def split(value):
    high = value.astype(jnp.bfloat16)
    return high, (value - high.astype(jnp.float32)).astype(jnp.bfloat16)


def operator_kernel(place, own, taken, passed, high, low):
    rows = own.shape[0]
    half = taken.shape[1]
    mid = rows // 2
    y_hi, z, core = place[0], place[1], place[2]
    first = pl.ds(pl.multiple_of(rows + core * mid, mid), mid)
    second = pl.ds(pl.multiple_of(rows + (1 - core) * mid, mid), mid)
    for d in range(NZ):
        source = pl.multiple_of(lax.rem(z + d, NZ) * rows, rows)
        target = pl.ds(d * rows, rows)
        here = own[:, pl.ds(pl.multiple_of(y_hi * half + source, rows), rows)]
        high[:rows, target], low[:rows, target] = split(here)
        high[first, target], low[first, target] = split(taken[:, pl.ds(source, rows)])
        high[second, target], low[second, target] = split(passed[:, pl.ds(source, rows)])


def inter_kernel(op_high, op_low, beta_part, *refs):
    blocks, (out, high, low) = refs[:-3], refs[-3:]
    rows = beta_part.shape[0]
    at = 0
    for ref in blocks:
        size = ref.shape[0]
        high[at:at + size, :], low[at:at + size, :] = split(ref[...])
        at += size

    def product(left, right):
        return jnp.dot(left[...], right[...], preferred_element_type=jnp.float32)

    out[...] = product(op_high, high) + (product(op_high, low) + product(op_low, high))
    out[:rows, :] += beta_part[...]


def term_kernel(coefficient, op_high, op_low, own, sent, here, *refs):
    pieces, (high, low) = refs[:-2], refs[-2:]
    rows = own.shape[0] // 2
    upper = coefficient[0] * (own[:rows, :] + sent[rows:, :])
    lower = coefficient[0] * (own[rows:, :] + sent[:rows, :])
    here[...] = upper
    high[:rows, :], low[:rows, :] = split(upper)
    high[rows:, :], low[rows:, :] = split(lower)

    def product(left, right):
        return lax.dot_general(
            left, right, (((0,), (0,)), ((), ())), preferred_element_type=jnp.float32
        )

    at = 0
    for piece in pieces:
        span = slice(at, at + piece.shape[0])
        piece[...] = product(op_high[:, span], high[...]) + (
            product(op_high[:, span], low[...]) + product(op_low[:, span], high[...])
        )
        at += piece.shape[0]


VMEM = pl.BlockSpec(memory_space=pltpu.VMEM)
SMEM = pl.BlockSpec(memory_space=pltpu.SMEM)


def call(kernel, outputs, operands, specs, scratch, flops):
    moved = sum(a.size * a.dtype.itemsize for a in operands)
    moved += sum(o.size * o.dtype.itemsize for o in outputs)
    return pl.pallas_call(
        kernel,
        out_shape=outputs,
        in_specs=specs,
        out_specs=[VMEM] * len(outputs),
        scratch_shapes=scratch,
        compiler_params=pltpu.CompilerParams(vmem_limit_bytes=40 * 2**20),
        cost_estimate=pl.CostEstimate(flops=flops, bytes_accessed=moved, transcendentals=0),
    )(*operands)


def on_device(
    vector, op_alpha, op_beta, op_weight, alpha_string, beta_string, alpha_energy, beta_energy
):
    rows, width = vector.shape
    quarter = width // 4
    pair = 2 * quarter
    half = NZ * rows
    mid = rows // 2
    alpha, beta, x = (lax.axis_index(name) for name in AXES)
    y_hi, z, odd = alpha // NZ, alpha % NZ, x % 2
    alpha_rows = op_alpha[0]
    beta_rows = op_beta[0]
    coefficient = 0.5 * op_weight[x]

    def columns(array, index):
        return lax.dynamic_slice_in_dim(array, index * quarter, quarter, 1)

    def near_of(array):
        return jnp.concatenate([columns(array, odd), columns(array, odd + 2)], 1)

    def far_of(array):
        return jnp.concatenate([columns(array, 1 - odd), columns(array, 3 - odd)], 1)

    def natural(near, far):
        parts = [near[:, :quarter], far[:, :quarter], near[:, quarter:], far[:, quarter:]]
        even = jnp.concatenate(parts, 1)
        swapped = jnp.concatenate([parts[1], parts[0], parts[3], parts[2]], 1)
        return jnp.where(odd == 0, even, swapped)

    start = near_of(vector)
    up1, down1 = move(start, dz=1), move(start, dz=-1)
    core = beta % 2
    give = lax.dynamic_slice(alpha_rows, (core * mid, (1 - y_hi) * half), (mid, half))
    taken = move(give, flip_hi=1, flip_lo=1)
    beta_low, beta_core = move(vector, flip_lo=1), move(vector, flip_core=1)
    far_up1, far_down1 = move(up1, dx=-1), move(down1, dx=1)
    up2, down2 = move(up1, dz=1), move(down1, dz=-1)
    far_up2, far_down2 = move(up2, dx=-1), move(down2, dx=1)
    up3, down3 = move(up2, dz=1), move(down2, dz=-1)
    up3, down3, far_up1, far_down1, beta_low, taken = together(
        up3, down3, far_up1, far_down1, beta_low, taken
    )
    passed = move(taken, flip_core=1)
    beta_both = move(beta_low, flip_core=1)
    far_up3, far_down3 = move(up3, dx=-1), move(down3, dx=1)
    up4, down4 = move(up3[:mid], dz=1), move(down3[mid:], dz=-1)
    vector_beta = dot(
        side_by_side(beta, vector, beta_core, beta_low, beta_both), beta_rows, 1, 1
    )
    place = jnp.stack([y_hi, z, core]).astype(jnp.int32)
    up4, down4, far_up2, far_down2, far_up3, far_down3, vector_beta, place, passed = together(
        up4, down4, far_up2, far_down2, far_up3, far_down3, vector_beta, place, passed
    )
    far_up4, far_down4 = move(up4, dx=-1), move(down4, dx=1)
    near_blocks = [start, down1, down2, down3, up4, down4, up3, up2, up1]
    far_blocks = [
        far_of(vector), far_down1, far_down2, far_down3, far_up4, far_down4, far_up3, far_up2, far_up1
    ]

    split_shape = jax.ShapeDtypeStruct((2 * rows, half), jnp.bfloat16)
    op_high, op_low = call(
        operator_kernel, [split_shape, split_shape], [place, alpha_rows, taken, passed], [SMEM, VMEM, VMEM, VMEM], [], 0
    )

    def share_of(blocks, beta_part):
        operands = [op_high, op_low, beta_part, *blocks]
        return call(
            inter_kernel,
            [jax.ShapeDtypeStruct((2 * rows, pair), jnp.float32)],
            operands,
            [VMEM] * len(operands),
            [pltpu.VMEM((half, pair), jnp.bfloat16)] * 2,
            6 * 2 * rows * half * pair,
        )[0]

    def terms_of(share, sizes):
        sent = move(share, flip_hi=1)
        operands = [coefficient.reshape(1), op_high, op_low, share, sent]
        return call(
            term_kernel,
            [jax.ShapeDtypeStruct((size, pair), jnp.float32) for size in (rows, *sizes)],
            operands,
            [SMEM] + [VMEM] * 4,
            [pltpu.VMEM((2 * rows, pair), jnp.bfloat16)] * 2,
            6 * 2 * rows * half * pair,
        )

    sizes = (rows, 2 * rows, rows + mid, rows + mid, 2 * rows)
    near_share = share_of(near_blocks, near_of(vector_beta))
    far_share = share_of(far_blocks, far_of(vector_beta))
    near_here, near_own, near_12, near_34, near_45, near_67 = terms_of(near_share, sizes)
    upper = move(near_34, dx=1)
    lower = move(near_45, dx=-1)
    upper_rest = move(near_12, dx=1)
    lower_rest = move(near_67, dx=-1)
    far_here, far_own, far_12, far_34, far_45, far_67 = terms_of(far_share, sizes)

    inter_rows = natural(near_here, far_here)
    inter_core, inter_low = move(inter_rows, flip_core=1), move(inter_rows, flip_lo=1)
    none = jnp.zeros((mid, pair), jnp.float32)
    up = move(far_34[rows:] + upper[rows:], dz=1)
    down = move(far_45[:mid] + lower[:mid], dz=-1)
    up, down = together(up, down)
    up = move(far_34[:rows] + upper[:rows] + jnp.concatenate([up, none], 0), dz=1)
    down = move(far_45[mid:] + lower[mid:] + jnp.concatenate([none, down], 0), dz=-1)
    up, down, inter_low = together(up, down, inter_low)
    inter_both = move(inter_low, flip_core=1)
    up = move(far_12[rows:] + upper_rest[rows:] + up, dz=1)
    down = move(far_67[:rows] + lower_rest[:rows] + down, dz=-1)
    inter_whole = side_by_side(beta, inter_rows, inter_core, inter_low, inter_both)
    up, down, inter_whole = together(up, down, inter_whole)
    up = move(far_12[:rows] + upper_rest[:rows] + up, dz=1)
    down = move(far_67[rows:] + lower_rest[rows:] + down, dz=-1)
    arrived = up + down

    inter_beta = dot(inter_whole, beta_rows, 1, 1)
    own = inter_beta + natural(near_own, far_own)
    opposite = move(columns(own, (x + 2) % 4), dx=2)
    swap = (x == 1) | (x == 2)
    low, high = arrived[:, :quarter], arrived[:, quarter:]
    right = jnp.where(swap, high, low) + columns(own, (x + 1) % 4)
    left = jnp.where(swap, low, high) + columns(own, (x + 3) % 4)
    total = columns(own, x) + move(right, dx=1) + move(left, dx=-1) + opposite

    own_strings = lax.dynamic_slice_in_dim(beta_string, x * quarter, quarter, 0)
    diag = alpha_energy[alpha_string][:, None] + beta_energy[own_strings][None, :]
    return total + diag * columns(vector, x)


def solution(mesh):
    return jax.shard_map(
        on_device,
        mesh=mesh,
        in_specs=(
            P("alpha", "beta"),
            P("task", "alpha", None),
            P("task", "beta", None),
            P(),
            P("alpha"),
            P("beta"),
            P(),
            P(),
        ),
        out_specs=P("alpha", ("beta", "task")),
        check_vma=False,
    )
```
